32 devices in a mesh: groups: 2 (over y), section: 4 (over z), dp: 2 (over x), space: 2 (over core).
Axes of the slice: x: 2, y: 2, z: 4, core: 2. Of those that a mesh axis runs over, the one named last changes fastest.
Arguments:
- images: bfloat16 [8, 16, 16, 256], P(('groups', 'dp'), 'space'), parts along dimension 0, may hold values from -6 to 6
- timesteps: int32 [8], P(('groups', 'dp')), parts along dimension 0, may hold values from 0 to 999
- time_embed: float32 [1000, 256], replicated, may hold values from -3 to 3
- conv_weight: bfloat16 [4, 2, 2304, 256], P('section'), may hold values from -0.125 to 0.125
- norm_gain: float32 [4, 2, 256], P('section'), may hold values from 0.1 to 1.9
- out_grad: bfloat16 [8, 16, 16, 256], P(('groups', 'dp'), 'space'), parts along dimension 0, may hold values from -6 to 6
Outputs:
- weight_grad: float32 [8, 2, 2304, 256], P(('groups', 'section'), None, ('dp', 'space')), parts along dimension 0
The draws below stay inside these ranges and needn't reach their ends.
There are 2 independent parts, one for each index of `groups`. The reference program is written for one: setup_inputs(seed, part) draws one part's arguments, and reference() takes and returns one part's arrays. A program takes and returns all parts, laid end to end along the dimension named above; an argument that names none is the same for every part. Nothing has to cross between parts.
All inputs are finite; a program needn't handle non-finite values.
Results may differ from the reference program's by a relative error of at most 0.013.
Values may be sent and summed in bfloat16 or wider, within the bound.
A program may use at most 64 MiB of HBM per device.

```python
import math
import jax
import jax.numpy as jnp
from jax import lax

C = 256
NT = 1000
MICRO = 2
ROWS_DEV = 8
COLS = 16
SECTIONS = 4
IMAGES = 4
HEIGHT = 16
N_SECTION = 4
N_DP = 2
N_SPACE = 2


def place_ends(values, key, smallest, top_value):
    longest = values.shape.index(max(values.shape))
    spots = []
    for shift in (0, 1):
        where = [jax.random.randint(jax.random.fold_in(key, axis), (), 0, length) for axis, length in enumerate(values.shape)]
        where[longest] = (where[longest] + shift) % values.shape[longest]
        spots.append(tuple(where))
    return values.at[spots[0]].set(smallest).at[spots[1]].set(top_value)


def block_levels(rng, dims, shards, smallest, high):
    def one(position, blocks):
        heights = jax.random.uniform(jax.random.fold_in(jax.random.fold_in(rng, 6), position), (blocks,), jnp.float32, smallest / len(shards), high / len(shards))
        return jnp.repeat(jnp.exp(heights), dims[position] // blocks).reshape((-1,) + (1,) * (len(dims) - position - 1))

    gain = one(*shards[0])
    for cut in shards[1:]:
        gain = gain * one(*cut)
    return gain


def scatter_about(key, dims, scale, reach, shards=(), kind=jnp.bfloat16):
    drawn = jax.random.normal(key, dims, jnp.float32) * scale
    if len(shards) > 0:
        drawn = block_levels(key, dims, shards, -0.22, 0.18) * drawn
    return jnp.clip(drawn, min=-reach, max=reach).astype(kind)


def setup_inputs(seed: int = 0, part: int = 0) -> dict:
    key_list = jax.random.split(jax.random.key(seed), 7)
    own_keys = jax.random.split(jax.random.fold_in(key_list[6], part), 7)
    images = scatter_about(own_keys[0], (IMAGES, HEIGHT, COLS, C), 1.0, 6.0, ((0, 2), (1, 2)))
    timesteps = place_ends(jax.random.randint(own_keys[1], (IMAGES,), 0, NT), jax.random.fold_in(own_keys[1], 1), 0, NT - 1).astype(jnp.int32)
    time_embed = scatter_about(key_list[2], (NT, C), 0.5, 3.0, (), jnp.float32)
    conv_weight = scatter_about(key_list[3], (SECTIONS, 2, 9 * C, C), (9 * C) ** -0.5, 0.125, ((0, 4),))
    norm_gain = jnp.clip(1.0 + 0.18 * jax.random.normal(key_list[4], (SECTIONS, 2, C), jnp.float32), 0.1, 1.9)
    out_grad = scatter_about(own_keys[5], (IMAGES, HEIGHT, COLS, C), 1.0, 6.0, ((0, 2), (1, 2)))
    return {"images": images, "timesteps": timesteps, "time_embed": time_embed, "conv_weight": conv_weight, "norm_gain": norm_gain, "out_grad": out_grad}


EPSILON = 1e-06

def normalize(values_in, gain_row, modulation):
    mean_sq = lax.optimization_barrier(jnp.mean(values_in * values_in, axis=-1, keepdims=True))
    return jax.nn.silu(values_in * lax.rsqrt(mean_sq + EPSILON) * (gain_row * modulation))

def conv_taps(padded):
    band_rows = padded.shape[-3] - 2
    band_cols = padded.shape[-2]
    widths = [(0, 0)] * (padded.ndim - 2) + [(1, 1), (0, 0)]
    framed = jnp.pad(padded, widths)
    tap_stack = [framed[..., row_off:row_off + band_rows, col_off:col_off + band_cols, :] for row_off in range(3) for col_off in range(3)]
    return jnp.concatenate(tap_stack, axis=-1)

def fold_taps(grad_taps, channels):
    band_rows, band_cols = (grad_taps.shape[-3], grad_taps.shape[-2])
    leading = grad_taps.shape[:-3]
    pieces = grad_taps.reshape(leading + (band_rows, band_cols, 9, channels))
    folded = jnp.zeros(leading + (band_rows + 2, band_cols + 2, channels), jnp.float32)
    for tap_index in range(9):
        row_off, col_off = (tap_index // 3, tap_index % 3)
        widths = [(0, 0)] * len(leading) + [(row_off, 2 - row_off), (col_off, 2 - col_off), (0, 0)]
        folded = folded + jnp.pad(pieces[..., tap_index, :], widths)
    return folded[..., 1:-1, :]

def apply_conv(tap_stack, weight):
    flat_rows = tap_stack.reshape(-1, tap_stack.shape[-1])
    result = jnp.dot(flat_rows, weight, preferred_element_type=jnp.float32)
    return result.reshape(tap_stack.shape[:-1] + (weight.shape[-1],))

def block_forward(a_pad, v_pad, weights, norm_gains, modulation, gated):
    f_main = normalize(a_pad.astype(jnp.float32), norm_gains[0], modulation).astype(jnp.bfloat16)
    f_side = normalize(v_pad.astype(jnp.float32), norm_gains[1], modulation).astype(jnp.bfloat16)
    p_main = apply_conv(conv_taps(f_main), weights[0])
    q_side = apply_conv(conv_taps(f_side), weights[1])
    centre = a_pad[..., 1:-1, :, :].astype(jnp.float32)
    mixed = jnp.where(gated, centre + p_main * jax.nn.sigmoid(q_side), centre + p_main + q_side)
    return (mixed.astype(jnp.bfloat16), p_main, q_side)

def block_backward(grad_out, a_pad, v_pad, p_main, q_side, weights, norm_gains, modulation, gated):
    f_main, pull_main = jax.vjp(lambda field_in: normalize(field_in, norm_gains[0], modulation), a_pad.astype(jnp.float32))
    f_side, pull_side = jax.vjp(lambda field_in: normalize(field_in, norm_gains[1], modulation), v_pad.astype(jnp.float32))
    taps_main = conv_taps(f_main.astype(jnp.bfloat16))
    taps_side = conv_taps(f_side.astype(jnp.bfloat16))
    gate_sig = jax.nn.sigmoid(q_side)
    back_main = jnp.where(gated, grad_out * gate_sig, grad_out).astype(jnp.bfloat16)
    back_side = jnp.where(gated, grad_out * p_main * gate_sig * (1.0 - gate_sig), grad_out).astype(jnp.bfloat16)
    channels = grad_out.shape[-1]
    grad_main = pull_main(fold_taps(apply_conv(back_main, weights[0].T), channels))[0]
    grad_side = pull_side(fold_taps(apply_conv(back_side, weights[1].T), channels))[0]
    widths = [(0, 0)] * (grad_out.ndim - 3) + [(1, 1), (0, 0), (0, 0)]
    grad_main = grad_main + jnp.pad(grad_out, widths)
    grad_input = jnp.where(gated, grad_main + grad_side, grad_main)
    grad_skip = jnp.where(gated, jnp.zeros_like(grad_side), grad_side)
    return (grad_input, grad_skip, taps_main, back_main, taps_side, back_side)

def settle(values_in):
    return lax.optimization_barrier(values_in.astype(jnp.bfloat16)).astype(jnp.float32)

def grouped(tap_stack, grads_in):
    shaped_taps = tap_stack.astype(jnp.float32).reshape(N_DP, MICRO, N_SPACE, ROWS_DEV, COLS, tap_stack.shape[-1])
    shaped_grads = grads_in.astype(jnp.float32).reshape(N_DP, MICRO, N_SPACE, ROWS_DEV, COLS, grads_in.shape[-1])
    partials = jnp.einsum('rmhyxk,rmhyxc->rhkc', shaped_taps, shaped_grads, precision=lax.Precision.HIGHEST)
    rounded = lax.optimization_barrier(partials.astype(jnp.bfloat16)).astype(jnp.float32)
    return lax.optimization_barrier(jnp.sum(rounded, axis=(0, 1)))

def reference(images, timesteps, time_embed, conv_weight, norm_gain, out_grad):
    encoders = N_SECTION // 2
    modulation = (1.0 + time_embed[timesteps])[:, None, None, :]
    pad_rows = ((0, 0), (1, 1), (0, 0), (0, 0))
    hidden = images
    enc_records = []
    enc_outputs = []
    for block_index in range(encoders):
        section_index = 2 * block_index
        a_pad = jnp.pad(hidden, pad_rows)
        output, p_main, q_side = block_forward(a_pad, a_pad, conv_weight[section_index], norm_gain[section_index], modulation, True)
        enc_records.append((a_pad, p_main, q_side))
        enc_outputs.append(output)
        hidden = output
    dec_records = [None] * encoders
    for block_index in reversed(range(encoders)):
        section_index = 2 * block_index + 1
        a_pad = jnp.pad(hidden, pad_rows)
        s_pad = jnp.pad(enc_outputs[block_index], pad_rows)
        output, p_main, q_side = block_forward(a_pad, s_pad, conv_weight[section_index], norm_gain[section_index], modulation, False)
        dec_records[block_index] = (a_pad, s_pad, p_main, q_side)
        hidden = output
    loss_scale = 1.0 / math.sqrt(IMAGES * HEIGHT * COLS)
    grad_out = out_grad.astype(jnp.float32) * loss_scale
    results = [None] * N_SECTION
    skip_grads = [None] * encoders
    for block_index in range(encoders):
        section_index = 2 * block_index + 1
        a_pad, s_pad, p_main, q_side = dec_records[block_index]
        grad_input, grad_skip, taps_main, back_main, taps_side, back_side = block_backward(grad_out, a_pad, s_pad, p_main, q_side, conv_weight[section_index], norm_gain[section_index], modulation, False)
        results[section_index] = jnp.stack([grouped(taps_main, back_main), grouped(taps_side, back_side)])
        grad_input = grad_input[:, 1:-1]
        grad_skip = grad_skip[:, 1:-1]
        if block_index < encoders - 1:
            skip_grads[block_index] = settle(grad_skip)
            grad_out = settle(grad_input)
        else:
            grad_out = settle(grad_input + grad_skip)
    for block_index in reversed(range(encoders)):
        section_index = 2 * block_index
        if block_index < encoders - 1:
            grad_out = grad_out + skip_grads[block_index]
        a_pad, p_main, q_side = enc_records[block_index]
        grad_input, grad_skip, taps_main, back_main, taps_side, back_side = block_backward(grad_out, a_pad, a_pad, p_main, q_side, conv_weight[section_index], norm_gain[section_index], modulation, True)
        results[section_index] = jnp.stack([grouped(taps_main, back_main), grouped(taps_side, back_side)])
        grad_out = settle(grad_input[:, 1:-1])
    return jnp.stack(results)
```

```python
import functools
import math

import jax
import jax.numpy as jnp
from jax import lax
from jax.experimental import pallas as pl
from jax.experimental.pallas import tpu as pltpu
from jax.sharding import PartitionSpec as P

EPSILON = 1e-06
MESH = pl.DeviceIdType.MESH
X, SKIP, G, GSKIP = range(4)


def sigmoid(z):
    return 0.5 + 0.5 * jnp.tanh(0.5 * z)


def inv_rms(x):
    return lax.rsqrt(jnp.mean(x * x, axis=-1, keepdims=True) + EPSILON)


def normalize(x, gain):
    z = x * inv_rms(x) * gain
    return z * sigmoid(z)


def pull_back(x, gain, grad_f):
    r = inv_rms(x)
    xr = x * r
    z = xr * gain
    s = sigmoid(z)
    u = grad_f * (s * (1.0 + z * (1.0 - s))) * gain
    return r * (u - xr * jnp.mean(xr * u, axis=-1, keepdims=True))


def store_shifts(value, cols, ref, start):
    n = value.shape[0]
    col = lax.broadcasted_iota(jnp.int32, value.shape, 0) % cols
    before = jnp.where(col == 0, 0.0, pltpu.roll(value, 1, 0))
    after = jnp.where(col == cols - 1, 0.0, pltpu.roll(value, n - 1, 0))
    ref[0, start : start + n, :] = before.astype(jnp.bfloat16)
    ref[1, start : start + n, :] = value.astype(jnp.bfloat16)
    ref[2, start : start + n, :] = after.astype(jnp.bfloat16)


def kernel(
    sections, replicas, micro, rows, cols, ch, taps, own_taps, loss_scale,
    ts_ref, images, table, weight, gains, out_grad, result,
    framed, pq, yout, sout, grad_f, shift, w, wt, tab, gn, gain_mod,
    f_all, g_all, ft, gshift, acc,
    lsem, band_s, band_r, halo_s, halo_r, pq_s, pq_r, f_s, f_r, g_s, g_r,
):
    sec = lax.axis_index("section")
    d = lax.axis_index("dp")
    h = lax.axis_index("space")
    other = 1 - h
    block = sec // 2
    enc = sec % 2 == 0
    dec = jnp.logical_not(enc)
    first, last = sec == 0, sec == 1
    turn = block == sections // 2 - 1
    follow = jnp.where(enc, jnp.where(turn, sec + 1, sec + 2), jnp.where(last, 0, sec - 2))
    ahead = jnp.where(dec, jnp.where(turn, sec - 1, sec + 2), jnp.where(first, 1, sec - 2))
    pair = jnp.where(enc, sec + 1, sec - 1)
    use_skip = jnp.logical_and(dec, jnp.logical_not(turn))
    use_gskip = jnp.logical_and(enc, jnp.logical_not(turn))
    pixels = rows * cols
    frame = pixels + 2 * cols
    peers = replicas * 2
    me = d * 2 + h
    band = pl.ds(cols, pixels)
    halo_out = pl.multiple_of(h * (pixels + cols), cols)
    halo_in = pl.multiple_of(other * (pixels + cols), cols)
    edge = pl.multiple_of(other * (pixels - cols), cols)

    def local(src, dst, i):
        return pltpu.make_async_copy(src, dst, lsem.at[i])

    def image_copy(m):
        return local(images.at[m], framed.at[X, m, band], m)

    def seed_copy(m):
        return local(out_grad.at[m], framed.at[G, m, band], micro + m)

    table_copy = local(table, tab, 2 * micro)
    gains_copy = local(gains, gn, 2 * micro + 1)
    weight_copy = local(weight, w, 2 * micro + 2)
    for m in range(micro):
        pl.when(first)(lambda m=m: image_copy(m).start())
        pl.when(last)(lambda m=m: seed_copy(m).start())
    table_copy.start()
    gains_copy.start()
    weight_copy.start()

    barrier = pltpu.get_barrier_semaphore()
    for s in (follow, ahead, pair):
        for side in range(2):
            pl.semaphore_signal(
                barrier, inc=1, device_id={"section": s, "space": side}, device_id_type=MESH
            )
    for k in range(1, peers):
        to = lax.rem(me + k, peers)
        pl.semaphore_signal(
            barrier, inc=1, device_id={"dp": to // 2, "space": to % 2}, device_id_type=MESH
        )

    zero_row = jnp.zeros((cols, ch), jnp.bfloat16)
    for m in range(micro):
        for kind in range(4):
            framed[kind, m, pl.ds(halo_out, cols), :] = zero_row
        for br in range(2):
            pq[m, br, pl.ds(halo_out, cols), :] = jnp.zeros((cols, ch), jnp.float32)
    for br in range(2):
        for k in range(3):
            gshift[br, k, 0:cols, :] = zero_row
            gshift[br, k, cols + 2 * pixels : 2 * cols + 2 * pixels, :] = zero_row
    acc[...] = jnp.zeros_like(acc)
    pl.semaphore_wait(barrier, 6 + peers - 1)

    def band_copy(kind, m, src, to):
        return pltpu.make_async_remote_copy(
            src, framed.at[kind, m, band], band_s.at[kind, m], band_r.at[kind, m],
            device_id={"section": to}, device_id_type=MESH,
        )

    def halo_copy(kind, m, src, to):
        return pltpu.make_async_remote_copy(
            src, framed.at[kind, m, pl.ds(halo_out, cols)],
            halo_s.at[kind, m], halo_r.at[kind, m],
            device_id={"section": to, "space": other}, device_id_type=MESH,
        )

    def sends(kind, m, src, to):
        return (
            halo_copy(kind, m, src.at[m, pl.ds(edge, cols)], to),
            band_copy(kind, m, src.at[m], to),
        )

    def rim_send(kind, m):
        src = framed.at[kind, m, pl.ds(pl.multiple_of(edge + cols, cols), cols)]
        return halo_copy(kind, m, src, sec)

    def band_wait(kind, m):
        band_copy(kind, m, yout.at[m], sec).wait_recv()

    def halo_wait(kind, m):
        pltpu.make_async_remote_copy(
            yout.at[m, pl.ds(0, cols)], framed.at[kind, m, pl.ds(halo_in, cols)],
            halo_s.at[kind, m], halo_r.at[kind, m],
            device_id={"section": sec, "space": other}, device_id_type=MESH,
        ).wait_recv()

    def pq_copy(m):
        return pltpu.make_async_remote_copy(
            pq.at[m, :, pl.ds(pl.multiple_of(edge + cols, cols), cols)],
            pq.at[m, :, pl.ds(halo_out, cols)],
            pq_s.at[m], pq_r.at[m], device_id={"space": other}, device_id_type=MESH,
        )

    def pq_wait(m):
        pltpu.make_async_remote_copy(
            pq.at[m, :, pl.ds(cols, cols)], pq.at[m, :, pl.ds(halo_in, cols)],
            pq_s.at[m], pq_r.at[m], device_id={"space": other}, device_id_type=MESH,
        ).wait_recv()

    def share(ref, send, recv, m, k):
        to = lax.rem(me + k, peers)
        return pltpu.make_async_remote_copy(
            ref.at[d * micro + m, h], ref.at[d * micro + m, h], send.at[k, m], recv.at[k, m],
            device_id={"dp": to // 2, "space": to % 2}, device_id_type=MESH,
        )

    def share_wait(ref, send, recv, m, k):
        source = lax.rem(me - k + peers, peers)
        slot = ref.at[source // 2 * micro + m, source % 2]
        pltpu.make_async_remote_copy(
            slot, slot, send.at[k, m], recv.at[k, m],
            device_id={"dp": source // 2, "space": source % 2}, device_id_type=MESH,
        ).wait_recv()

    def each_micro(body):
        lax.fori_loop(0, micro, lambda m, c: (body(m), c)[1], 0)

    def start_rims():
        def images_in(m):
            image_copy(m).wait()
            rim_send(X, m).start()

        def seeds_in(m):
            seed_copy(m).wait()
            rim_send(G, m).start()

        pl.when(first)(lambda: each_micro(images_in))
        pl.when(last)(lambda: each_micro(seeds_in))

    start_rims()
    table_copy.wait()
    gains_copy.wait()
    for m in range(micro):
        modulation = 1.0 + tab[pl.ds(ts_ref[m], 1), :]
        gain_mod[m, :, :] = gn[...] * modulation
    weight_copy.wait()

    def gain_of(m, br):
        return gain_mod[m, pl.ds(br, 1), :]

    def wait_inputs(m):
        pl.when(jnp.logical_not(first))(lambda: band_wait(X, m))
        halo_wait(X, m)

        @pl.when(use_skip)
        def _():
            band_wait(SKIP, m)
            halo_wait(SKIP, m)

    def inputs(m, part):
        a = framed[X, m, part, :].astype(jnp.float32)
        v = jnp.where(use_skip, framed[SKIP, m, part, :].astype(jnp.float32), a)
        return a, v

    def share_f(m):
        for k in range(1, peers):
            share(f_all, f_s, f_r, m, k).start()

    def share_g(m):
        for k in range(1, peers):
            share(g_all, g_s, g_r, m, k).start()

    def conv(kernels, br, backward):
        pieces = []
        for t in range(9):
            i, j = t // 3, t % 3
            if backward:
                i, j = 2 - i, 2 - j
            pieces.append(shift[br, j, i * cols : i * cols + pixels, :])
        lhs = jnp.concatenate(pieces, axis=1)
        return jnp.dot(lhs, kernels[br], preferred_element_type=jnp.float32)

    def forward(m):
        wait_inputs(m)
        a, v = inputs(m, pl.ds(0, frame))
        for br, x in ((0, a), (1, v)):
            f = normalize(x, gain_of(m, br))
            store_shifts(f, cols, shift.at[br], 0)
            f_all[d * micro + m, h, br, :, :] = shift[br, 1, cols : cols + pixels, :]
        p = conv(w, 0, False)
        q = conv(w, 1, False)
        centre = framed[X, m, band, :].astype(jnp.float32)
        y = jnp.where(enc, centre + p * sigmoid(q), centre + p + q)
        yout[m] = y.astype(jnp.bfloat16)
        for copy in sends(X, m, yout, follow):
            copy.start()

        @pl.when(use_gskip)
        def _():
            for copy in sends(SKIP, m, yout, pair):
                copy.start()

        pq[m, 0, band, :] = p
        pq[m, 1, band, :] = q
        pq_copy(m).start()
        share_f(m)

    def transposes():
        def one(t, c):
            at = pl.ds(pl.multiple_of(t * ch, ch), ch)
            for br in range(2):
                wt[br, at, :] = w[br, at, :].T
            return c

        lax.fori_loop(0, 9, one, 0)

    def field_grads(m):
        pl.when(jnp.logical_not(last))(lambda: band_wait(G, m))
        halo_wait(G, m)

        @pl.when(use_gskip)
        def _():
            band_wait(GSKIP, m)
            halo_wait(GSKIP, m)

        g = out_gradient(m, pl.ds(0, frame))
        s = sigmoid(pq[m, 1])
        gp = jnp.where(enc, g * s, g)
        gq = jnp.where(enc, g * pq[m, 0] * s * (1.0 - s), g)
        for br, grad in ((0, gp), (1, gq)):
            store_shifts(grad, cols, shift.at[br], 0)
            g_all[d * micro + m, h, br, :, :] = shift[br, 1, cols : cols + pixels, :]
        pl.when(first)(lambda: share_g(m))

        @pl.when(jnp.logical_not(first))
        def _():
            for br in range(2):
                grad_f[m, br] = conv(wt, br, True)

    def out_gradient(m, part):
        g = framed[G, m, part, :].astype(jnp.float32)
        g = g + jnp.where(use_gskip, framed[GSKIP, m, part, :].astype(jnp.float32), 0.0)
        return g * jnp.where(last, loss_scale, 1.0)

    def pass_grads(m):
        a, v = inputs(m, band)
        main = pull_back(a, gain_of(m, 0), grad_f[m, 0])
        side = pull_back(v, gain_of(m, 1), grad_f[m, 1])
        g = out_gradient(m, band)
        yout_g = g + main + jnp.where(use_skip, 0.0, side)
        sout[0, m] = yout_g.astype(jnp.bfloat16)
        for copy in sends(G, m, sout.at[0], ahead):
            copy.start()

        @pl.when(use_skip)
        def _():
            sout[1, m] = side.astype(jnp.bfloat16)
            for copy in sends(GSKIP, m, sout.at[1], pair):
                copy.start()

        share_g(m)

    def late_fields(m):
        a, v = inputs(m, band)
        for br, x in ((0, a), (1, v)):
            f_all[d * micro + m, h, br, :, :] = normalize(x, gain_of(m, br)).astype(jnp.bfloat16)
        share_f(m)

    def gather_fields():
        def one(m):
            for k in range(1, peers):
                share_wait(f_all, f_s, f_r, m, k)

            def flip(r, c):
                for br in range(2):
                    for side in range(2):
                        at = slice(side * pixels, (side + 1) * pixels)
                        ft[r * micro + m, br, :, at] = f_all[r * micro + m, side, br].T
                return c

            lax.fori_loop(0, replicas, flip, 0)

        each_micro(one)

    def last_section():
        transposes()
        each_micro(field_grads)

        def one(m):
            wait_inputs(m)
            pass_grads(m)

        each_micro(one)
        each_micro(late_fields)
        gather_fields()

    def other_sections():
        each_micro(forward)
        pl.when(jnp.logical_not(first))(transposes)
        each_micro(pq_wait)
        pl.when(enc)(gather_fields)

        def one(m):
            field_grads(m)
            pl.when(jnp.logical_not(first))(lambda: pass_grads(m))

        each_micro(one)
        pl.when(dec)(gather_fields)

    pl.when(last)(last_section)
    pl.when(jnp.logical_not(last))(other_sections)

    own = 9 * ch // peers
    tap0 = jnp.minimum(me * own // ch, 9 - own_taps)
    offset = pl.multiple_of(me * own - tap0 * ch, 16)

    def weight_terms(m):
        for k in range(1, peers):
            share_wait(g_all, g_s, g_r, m, k)

        def one(r, c):
            image = r * micro + m
            for br in range(2):
                for side in range(2):
                    store_shifts(
                        g_all[image, side, br].astype(jnp.float32),
                        cols, gshift.at[br], cols + side * pixels,
                    )
                for n in range(own_taps):
                    t = tap0 + n
                    start = pl.multiple_of((2 - t // 3) * cols, cols)
                    rhs = gshift[br, 2 - t % 3, pl.ds(start, 2 * pixels), :]
                    acc[br, n * ch : (n + 1) * ch, :] += jnp.dot(
                        ft[image, br], rhs, preferred_element_type=jnp.float32
                    )
            return c

        lax.fori_loop(0, replicas, one, 0)

    each_micro(weight_terms)
    out_copy = local(acc.at[:, pl.ds(offset, own)], result, 2 * micro + 3)
    out_copy.start()

    def finish(m):
        pl.when(first)(lambda: rim_send(X, m).wait_send())
        pl.when(last)(lambda: rim_send(G, m).wait_send())

        @pl.when(jnp.logical_not(last))
        def _():
            for copy in sends(X, m, yout, follow):
                copy.wait_send()
            pq_copy(m).wait_send()

        @pl.when(jnp.logical_not(first))
        def _():
            for copy in sends(G, m, sout.at[0], ahead):
                copy.wait_send()

        @pl.when(use_gskip)
        def _():
            for copy in sends(SKIP, m, yout, pair):
                copy.wait_send()

        @pl.when(use_skip)
        def _():
            for copy in sends(GSKIP, m, sout.at[1], pair):
                copy.wait_send()

        for k in range(1, peers):
            share(f_all, f_s, f_r, m, k).wait_send()
            share(g_all, g_s, g_r, m, k).wait_send()

    each_micro(finish)
    out_copy.wait()


def shards(images, timesteps, time_embed, conv_weight, norm_gain, out_grad):
    micro, rows, cols, ch = images.shape
    sections = lax.axis_size("section")
    replicas = lax.axis_size("dp")
    spaces = lax.axis_size("space")
    taps = conv_weight.shape[2]
    peers = replicas * spaces
    own = taps // peers
    own_taps = max(((n + 1) * own - 1) // ch - n * own // ch + 1 for n in range(peers))
    loss_scale = 1.0 / math.sqrt(micro * replicas * rows * spaces * cols)
    pixels = rows * cols
    frame = pixels + 2 * cols
    bf, f32 = jnp.bfloat16, jnp.float32
    dma = pltpu.SemaphoreType.DMA
    any_spec = pl.BlockSpec(memory_space=pl.ANY)
    result = pl.pallas_call(
        functools.partial(
            kernel, sections, replicas, micro, rows, cols, ch, taps, own_taps, loss_scale
        ),
        out_shape=jax.ShapeDtypeStruct((2, own, ch), f32),
        in_specs=[pl.BlockSpec(memory_space=pltpu.SMEM)] + [any_spec] * 5,
        out_specs=any_spec,
        scratch_shapes=[
            pltpu.VMEM((4, micro, frame, ch), bf),
            pltpu.VMEM((micro, 2, frame, ch), f32),
            pltpu.VMEM((micro, pixels, ch), bf),
            pltpu.VMEM((2, micro, pixels, ch), bf),
            pltpu.VMEM((micro, 2, pixels, ch), f32),
            pltpu.VMEM((2, 3, frame, ch), bf),
            pltpu.VMEM((2, taps, ch), bf),
            pltpu.VMEM((2, taps, ch), bf),
            pltpu.VMEM(time_embed.shape, f32),
            pltpu.VMEM((2, ch), f32),
            pltpu.VMEM((micro, 2, ch), f32),
            pltpu.VMEM((replicas * micro, 2, 2, pixels, ch), bf),
            pltpu.VMEM((replicas * micro, 2, 2, pixels, ch), bf),
            pltpu.VMEM((replicas * micro, 2, ch, 2 * pixels), bf),
            pltpu.VMEM((2, 3, 2 * pixels + 2 * cols, ch), bf),
            pltpu.VMEM((2, own_taps * ch, ch), f32),
            dma((2 * micro + 4,)),
            dma((4, micro)),
            dma((4, micro)),
            dma((4, micro)),
            dma((4, micro)),
            dma((micro,)),
            dma((micro,)),
            dma((peers, micro)),
            dma((peers, micro)),
            dma((peers, micro)),
            dma((peers, micro)),
        ],
        compiler_params=pltpu.CompilerParams(
            collective_id=0, has_side_effects=True, vmem_limit_bytes=48 * 2**20
        ),
    )(
        timesteps,
        images.reshape(micro, pixels, ch),
        time_embed,
        conv_weight[0],
        norm_gain[0],
        out_grad.reshape(micro, pixels, ch),
    )
    return result[None]


def solution(mesh):
    placed = (
        P(("groups", "dp"), "space", None, None),
        P(("groups", "dp")),
        P(),
        P("section", None, None, None),
        P("section", None, None),
        P(("groups", "dp"), "space", None, None),
    )
    return jax.shard_map(
        shards,
        mesh=mesh,
        in_specs=placed,
        out_specs=P(("groups", "section"), None, ("dp", "space"), None),
        check_vma=False,
    )
```

```python
import functools
import math

import jax
import jax.numpy as jnp
from jax import lax
from jax.experimental import pallas as pl
from jax.experimental.pallas import tpu as pltpu
from jax.sharding import PartitionSpec as P

EPSILON = 1e-06
MESH = pl.DeviceIdType.MESH
X, SKIP, G, GSKIP = range(4)


def sigmoid(z):
    return 0.5 + 0.5 * jnp.tanh(0.5 * z)


def inv_rms(x):
    return lax.rsqrt(jnp.mean(x * x, axis=-1, keepdims=True) + EPSILON)


def normalize(x, gain):
    z = x * inv_rms(x) * gain
    return z * sigmoid(z)


def pull_back(x, gain, grad_f):
    r = inv_rms(x)
    xr = x * r
    z = xr * gain
    s = sigmoid(z)
    u = grad_f * (s * (1.0 + z * (1.0 - s))) * gain
    return r * (u - xr * jnp.mean(xr * u, axis=-1, keepdims=True))


def store_shifts(value, cols, ref, start):
    n = value.shape[0]
    col = lax.broadcasted_iota(jnp.int32, value.shape, 0) % cols
    before = jnp.where(col == 0, 0.0, pltpu.roll(value, 1, 0))
    after = jnp.where(col == cols - 1, 0.0, pltpu.roll(value, n - 1, 0))
    ref[0, start : start + n, :] = before.astype(jnp.bfloat16)
    ref[1, start : start + n, :] = value.astype(jnp.bfloat16)
    ref[2, start : start + n, :] = after.astype(jnp.bfloat16)


def kernel(
    sections, replicas, micro, rows, cols, ch, taps, own_taps, loss_scale,
    ts_ref, images, table, weight, gains, out_grad, result,
    framed, gates, yout, sout, grad_f, shift, w, wt, tab, gn, gain_mod,
    f_all, ab_all, g_all, ft, gshift, acc,
    lsem, band_s, band_r, halo_s, halo_r, pq_s, pq_r, f_s, f_r, ab_s, ab_r, g_s, g_r,
):
    sec = lax.axis_index("section")
    d = lax.axis_index("dp")
    h = lax.axis_index("space")
    other = 1 - h
    block = sec // 2
    enc = sec % 2 == 0
    dec = jnp.logical_not(enc)
    first, last = sec == 0, sec == 1
    turn = block == sections // 2 - 1
    follow = jnp.where(enc, jnp.where(turn, sec + 1, sec + 2), jnp.where(last, 0, sec - 2))
    ahead = jnp.where(dec, jnp.where(turn, sec - 1, sec + 2), jnp.where(first, 1, sec - 2))
    pair = jnp.where(enc, sec + 1, sec - 1)
    use_skip = jnp.logical_and(dec, jnp.logical_not(turn))
    use_gskip = jnp.logical_and(enc, jnp.logical_not(turn))
    pixels = rows * cols
    frame = pixels + 2 * cols
    peers = replicas * 2
    me = d * 2 + h
    band = pl.ds(cols, pixels)
    halo_out = pl.multiple_of(h * (pixels + cols), cols)
    halo_in = pl.multiple_of(other * (pixels + cols), cols)
    edge = pl.multiple_of(other * (pixels - cols), cols)

    def local(src, dst, i):
        return pltpu.make_async_copy(src, dst, lsem.at[i])

    def image_copy(m):
        return local(images.at[m], framed.at[X, m, band], m)

    def seed_copy(m):
        return local(out_grad.at[m], framed.at[G, m, band], micro + m)

    table_copy = local(table, tab, 2 * micro)
    gains_copy = local(gains, gn, 2 * micro + 1)
    weight_copy = local(weight, w, 2 * micro + 2)
    for m in range(micro):
        pl.when(first)(lambda m=m: image_copy(m).start())
        pl.when(last)(lambda m=m: seed_copy(m).start())
    table_copy.start()
    gains_copy.start()
    weight_copy.start()

    barrier = pltpu.get_barrier_semaphore()
    for s in (follow, ahead, pair):
        for side in range(2):
            pl.semaphore_signal(
                barrier, inc=1, device_id={"section": s, "space": side}, device_id_type=MESH
            )
    for k in range(1, peers):
        to = lax.rem(me + k, peers)
        pl.semaphore_signal(
            barrier, inc=1, device_id={"dp": to // 2, "space": to % 2}, device_id_type=MESH
        )

    zero_row = jnp.zeros((cols, ch), jnp.bfloat16)
    for m in range(micro):
        for kind in range(4):
            framed[kind, m, pl.ds(halo_out, cols), :] = zero_row
        for br in range(2):
            gates[m, br, pl.ds(halo_out, cols), :] = jnp.zeros((cols, ch), jnp.float32)
    for br in range(2):
        for k in range(3):
            gshift[br, k, 0:cols, :] = zero_row
            gshift[br, k, cols + 2 * pixels : 2 * cols + 2 * pixels, :] = zero_row
    acc[...] = jnp.zeros_like(acc)
    pl.semaphore_wait(barrier, 6 + peers - 1)

    def band_copy(kind, m, src, to):
        return pltpu.make_async_remote_copy(
            src, framed.at[kind, m, band], band_s.at[kind, m], band_r.at[kind, m],
            device_id={"section": to}, device_id_type=MESH,
        )

    def halo_copy(kind, m, src, to):
        return pltpu.make_async_remote_copy(
            src, framed.at[kind, m, pl.ds(halo_out, cols)],
            halo_s.at[kind, m], halo_r.at[kind, m],
            device_id={"section": to, "space": other}, device_id_type=MESH,
        )

    def sends(kind, m, src, to):
        return (
            halo_copy(kind, m, src.at[m, pl.ds(edge, cols)], to),
            band_copy(kind, m, src.at[m], to),
        )

    def rim_send(kind, m):
        src = framed.at[kind, m, pl.ds(pl.multiple_of(edge + cols, cols), cols)]
        return halo_copy(kind, m, src, sec)

    def band_wait(kind, m):
        band_copy(kind, m, yout.at[m], sec).wait_recv()

    def halo_wait(kind, m):
        pltpu.make_async_remote_copy(
            yout.at[m, pl.ds(0, cols)], framed.at[kind, m, pl.ds(halo_in, cols)],
            halo_s.at[kind, m], halo_r.at[kind, m],
            device_id={"section": sec, "space": other}, device_id_type=MESH,
        ).wait_recv()

    def pq_copy(m):
        return pltpu.make_async_remote_copy(
            gates.at[m, :, pl.ds(pl.multiple_of(edge + cols, cols), cols)],
            gates.at[m, :, pl.ds(halo_out, cols)],
            pq_s.at[m], pq_r.at[m], device_id={"space": other}, device_id_type=MESH,
        )

    def pq_wait(m):
        pltpu.make_async_remote_copy(
            gates.at[m, :, pl.ds(cols, cols)], gates.at[m, :, pl.ds(halo_in, cols)],
            pq_s.at[m], pq_r.at[m], device_id={"space": other}, device_id_type=MESH,
        ).wait_recv()

    def share(ref, send, recv, m, k):
        to = lax.rem(me + k, peers)
        return pltpu.make_async_remote_copy(
            ref.at[d * micro + m, h], ref.at[d * micro + m, h], send.at[k, m], recv.at[k, m],
            device_id={"dp": to // 2, "space": to % 2}, device_id_type=MESH,
        )

    def share_wait(ref, send, recv, m, r):
        def one(side):
            source = r * 2 + side
            k = lax.rem(me - source + peers, peers)
            slot = ref.at[r * micro + m, side]
            pltpu.make_async_remote_copy(
                slot, slot, send.at[k, m], recv.at[k, m],
                device_id={"dp": r, "space": side}, device_id_type=MESH,
            ).wait_recv()

        one(other)
        pl.when(r != d)(lambda: one(h))

    def each_micro(body):
        lax.fori_loop(0, micro, lambda m, c: (body(m), c)[1], 0)

    def start_rims():
        def images_in(m):
            image_copy(m).wait()
            rim_send(X, m).start()

        def seeds_in(m):
            seed_copy(m).wait()
            rim_send(G, m).start()

        pl.when(first)(lambda: each_micro(images_in))
        pl.when(last)(lambda: each_micro(seeds_in))

    start_rims()
    table_copy.wait()
    gains_copy.wait()
    for m in range(micro):
        modulation = 1.0 + tab[pl.ds(ts_ref[m], 1), :]
        gain_mod[m, :, :] = gn[...] * modulation
    weight_copy.wait()

    def gain_of(m, br):
        return gain_mod[m, pl.ds(br, 1), :]

    def wait_inputs(m):
        pl.when(jnp.logical_not(first))(lambda: band_wait(X, m))
        halo_wait(X, m)

        @pl.when(use_skip)
        def _():
            band_wait(SKIP, m)
            halo_wait(SKIP, m)

    def inputs(m, part):
        a = framed[X, m, part, :].astype(jnp.float32)
        v = jnp.where(use_skip, framed[SKIP, m, part, :].astype(jnp.float32), a)
        return a, v

    def share_f(m):
        for k in range(1, peers):
            share(f_all, f_s, f_r, m, k).start()

    def share_g(m):
        for k in range(1, peers):
            share(g_all, g_s, g_r, m, k).start()

    def conv(kernels, br, backward):
        pieces = []
        for t in range(9):
            i, j = t // 3, t % 3
            if backward:
                i, j = 2 - i, 2 - j
            pieces.append(shift[br, j, i * cols : i * cols + pixels, :])
        lhs = jnp.concatenate(pieces, axis=1)
        return jnp.dot(lhs, kernels[br], preferred_element_type=jnp.float32)

    def forward(m):
        wait_inputs(m)
        a, v = inputs(m, pl.ds(0, frame))
        for br, x in ((0, a), (1, v)):
            f = normalize(x, gain_of(m, br))
            store_shifts(f, cols, shift.at[br], 0)
            f_all[d * micro + m, h, br, :, :] = shift[br, 1, cols : cols + pixels, :]
        p = conv(w, 0, False)
        q = conv(w, 1, False)
        centre = framed[X, m, band, :].astype(jnp.float32)
        y = jnp.where(enc, centre + p * sigmoid(q), centre + p + q)
        yout[m] = y.astype(jnp.bfloat16)
        for copy in sends(X, m, yout, follow):
            copy.start()

        @pl.when(use_gskip)
        def _():
            for copy in sends(SKIP, m, yout, pair):
                copy.start()

        share_f(m)

        @pl.when(enc)
        def _():
            slot = d * micro + m
            s = sigmoid(q)
            for br, gate in ((0, s), (1, p * s * (1.0 - s))):
                gates[m, br, band, :] = gate
                ab_all[slot, h, br, :, :] = gate.astype(jnp.bfloat16)
            pq_copy(m).start()
            for k in range(1, peers):
                share(ab_all, ab_s, ab_r, m, k).start()

    def transposes():
        def one(t, c):
            at = pl.ds(pl.multiple_of(t * ch, ch), ch)
            for br in range(2):
                wt[br, at, :] = w[br, at, :].T
            return c

        lax.fori_loop(0, 9, one, 0)

    def field_grads(m):
        pl.when(jnp.logical_not(last))(lambda: band_wait(G, m))
        halo_wait(G, m)

        @pl.when(use_gskip)
        def _():
            band_wait(GSKIP, m)
            halo_wait(GSKIP, m)

        g = out_gradient(m, pl.ds(0, frame))
        g_all[d * micro + m, h, :, :] = g[cols : cols + pixels].astype(jnp.bfloat16)
        pl.when(first)(lambda: share_g(m))

        @pl.when(jnp.logical_not(first))
        def _():
            for br in range(2):
                grad = jnp.where(enc, g * gates[m, br], g)
                store_shifts(grad, cols, shift.at[br], 0)
            for br in range(2):
                grad_f[m, br] = conv(wt, br, True)

    def out_gradient(m, part):
        g = framed[G, m, part, :].astype(jnp.float32)
        g = g + jnp.where(use_gskip, framed[GSKIP, m, part, :].astype(jnp.float32), 0.0)
        return g * jnp.where(last, loss_scale, 1.0)

    def pass_grads(m):
        a, v = inputs(m, band)
        main = pull_back(a, gain_of(m, 0), grad_f[m, 0])
        side = pull_back(v, gain_of(m, 1), grad_f[m, 1])
        g = out_gradient(m, band)
        yout_g = g + main + jnp.where(use_skip, 0.0, side)
        sout[0, m] = yout_g.astype(jnp.bfloat16)
        for copy in sends(G, m, sout.at[0], ahead):
            copy.start()

        @pl.when(use_skip)
        def _():
            sout[1, m] = side.astype(jnp.bfloat16)
            for copy in sends(GSKIP, m, sout.at[1], pair):
                copy.start()

        share_g(m)

    def late_fields(m):
        a, v = inputs(m, band)
        for br, x in ((0, a), (1, v)):
            f_all[d * micro + m, h, br, :, :] = normalize(x, gain_of(m, br)).astype(jnp.bfloat16)
        share_f(m)

    def gather_fields():
        def one(m):
            def flip(rr, c):
                r = lax.rem(d + rr, replicas)
                share_wait(f_all, f_s, f_r, m, r)
                pl.when(enc)(lambda: share_wait(ab_all, ab_s, ab_r, m, r))
                for br in range(2):
                    for side in range(2):
                        at = slice(side * pixels, (side + 1) * pixels)
                        ft[r * micro + m, br, :, at] = f_all[r * micro + m, side, br].T
                return c

            lax.fori_loop(0, replicas, flip, 0)

        each_micro(one)

    def last_section():
        transposes()
        each_micro(field_grads)

        def one(m):
            wait_inputs(m)
            pass_grads(m)

        each_micro(one)
        each_micro(late_fields)
        gather_fields()

    def other_sections():
        each_micro(forward)
        pl.when(jnp.logical_not(first))(transposes)
        pl.when(enc)(lambda: each_micro(pq_wait))
        pl.when(enc)(gather_fields)

        def one(m):
            field_grads(m)
            pl.when(jnp.logical_not(first))(lambda: pass_grads(m))

        each_micro(one)
        pl.when(dec)(gather_fields)

    pl.when(last)(last_section)
    pl.when(jnp.logical_not(last))(other_sections)

    own = 9 * ch // peers
    tap0 = jnp.minimum(me * own // ch, 9 - own_taps)
    offset = pl.multiple_of(me * own - tap0 * ch, 16)

    def weight_terms(m):
        def one(rr, c):
            r = lax.rem(d + rr, replicas)
            image = r * micro + m
            share_wait(g_all, g_s, g_r, m, r)
            for br in range(2):
                for side in range(2):
                    g = g_all[image, side].astype(jnp.float32)
                    gate = ab_all[image, side, br].astype(jnp.float32)
                    grad = jnp.where(enc, g * gate, g)
                    store_shifts(grad, cols, gshift.at[br], cols + side * pixels)
            for br in range(2):
                for n in range(own_taps):
                    t = tap0 + n
                    start = pl.multiple_of((2 - t // 3) * cols, cols)
                    rhs = gshift[br, 2 - t % 3, pl.ds(start, 2 * pixels), :]
                    acc[br, n * ch : (n + 1) * ch, :] += jnp.dot(
                        ft[image, br], rhs, preferred_element_type=jnp.float32
                    )
            return c

        lax.fori_loop(0, replicas, one, 0)

    each_micro(weight_terms)
    out_copy = local(acc.at[:, pl.ds(offset, own)], result, 2 * micro + 3)
    out_copy.start()

    def finish(m):
        pl.when(first)(lambda: rim_send(X, m).wait_send())
        pl.when(last)(lambda: rim_send(G, m).wait_send())

        @pl.when(jnp.logical_not(last))
        def _():
            for copy in sends(X, m, yout, follow):
                copy.wait_send()

        @pl.when(enc)
        def _():
            pq_copy(m).wait_send()
            for k in range(1, peers):
                share(ab_all, ab_s, ab_r, m, k).wait_send()

        @pl.when(jnp.logical_not(first))
        def _():
            for copy in sends(G, m, sout.at[0], ahead):
                copy.wait_send()

        @pl.when(use_gskip)
        def _():
            for copy in sends(SKIP, m, yout, pair):
                copy.wait_send()

        @pl.when(use_skip)
        def _():
            for copy in sends(GSKIP, m, sout.at[1], pair):
                copy.wait_send()

        for k in range(1, peers):
            share(f_all, f_s, f_r, m, k).wait_send()
            share(g_all, g_s, g_r, m, k).wait_send()

    each_micro(finish)
    out_copy.wait()


def shards(images, timesteps, time_embed, conv_weight, norm_gain, out_grad):
    micro, rows, cols, ch = images.shape
    sections = lax.axis_size("section")
    replicas = lax.axis_size("dp")
    spaces = lax.axis_size("space")
    taps = conv_weight.shape[2]
    peers = replicas * spaces
    own = taps // peers
    own_taps = max(((n + 1) * own - 1) // ch - n * own // ch + 1 for n in range(peers))
    loss_scale = 1.0 / math.sqrt(micro * replicas * rows * spaces * cols)
    pixels = rows * cols
    frame = pixels + 2 * cols
    bf, f32 = jnp.bfloat16, jnp.float32
    dma = pltpu.SemaphoreType.DMA
    any_spec = pl.BlockSpec(memory_space=pltpu.HBM)
    result = pl.pallas_call(
        functools.partial(
            kernel, sections, replicas, micro, rows, cols, ch, taps, own_taps, loss_scale
        ),
        out_shape=jax.ShapeDtypeStruct((2, own, ch), f32),
        in_specs=[pl.BlockSpec(memory_space=pltpu.SMEM)] + [any_spec] * 5,
        out_specs=any_spec,
        scratch_shapes=[
            pltpu.VMEM((4, micro, frame, ch), bf),
            pltpu.VMEM((micro, 2, frame, ch), f32),
            pltpu.VMEM((micro, pixels, ch), bf),
            pltpu.VMEM((2, micro, pixels, ch), bf),
            pltpu.VMEM((micro, 2, pixels, ch), f32),
            pltpu.VMEM((2, 3, frame, ch), bf),
            pltpu.VMEM((2, taps, ch), bf),
            pltpu.VMEM((2, taps, ch), bf),
            pltpu.VMEM(time_embed.shape, f32),
            pltpu.VMEM((2, ch), f32),
            pltpu.VMEM((micro, 2, ch), f32),
            pltpu.VMEM((replicas * micro, 2, 2, pixels, ch), bf),
            pltpu.VMEM((replicas * micro, 2, 2, pixels, ch), bf),
            pltpu.VMEM((replicas * micro, 2, pixels, ch), bf),
            pltpu.VMEM((replicas * micro, 2, ch, 2 * pixels), bf),
            pltpu.VMEM((2, 3, 2 * pixels + 2 * cols, ch), bf),
            pltpu.VMEM((2, own_taps * ch, ch), f32),
            dma((2 * micro + 4,)),
            dma((4, micro)),
            dma((4, micro)),
            dma((4, micro)),
            dma((4, micro)),
            dma((micro,)),
            dma((micro,)),
            dma((peers, micro)),
            dma((peers, micro)),
            dma((peers, micro)),
            dma((peers, micro)),
            dma((peers, micro)),
            dma((peers, micro)),
        ],
        compiler_params=pltpu.CompilerParams(
            collective_id=0, has_side_effects=True, vmem_limit_bytes=60 * 2**20
        ),
    )(
        timesteps,
        images.reshape(micro, pixels, ch),
        time_embed,
        conv_weight[0],
        norm_gain[0],
        out_grad.reshape(micro, pixels, ch),
    )
    return result[None]


def solution(mesh):
    placed = (
        P(("groups", "dp"), "space", None, None),
        P(("groups", "dp")),
        P(),
        P("section", None, None, None),
        P("section", None, None),
        P(("groups", "dp"), "space", None, None),
    )
    return jax.shard_map(
        shards,
        mesh=mesh,
        in_specs=placed,
        out_specs=P(("groups", "section"), None, ("dp", "space"), None),
        check_vma=False,
    )
```

```python
import functools
import math

import jax
import jax.numpy as jnp
from jax import lax
from jax.experimental import pallas as pl
from jax.experimental.pallas import tpu as pltpu
from jax.sharding import PartitionSpec as P

EPSILON = 1e-06
MESH = pl.DeviceIdType.MESH
X, SKIP, G, GSKIP = range(4)


def sigmoid(z):
    return 0.5 + 0.5 * jnp.tanh(0.5 * z)


def inv_rms(x):
    return lax.rsqrt(jnp.mean(x * x, axis=-1, keepdims=True) + EPSILON)


def normalize(x, gain):
    z = x * inv_rms(x) * gain
    return z * sigmoid(z)


def pull_back(x, gain, grad_f):
    r = inv_rms(x)
    xr = x * r
    z = xr * gain
    s = sigmoid(z)
    u = grad_f * (s * (1.0 + z * (1.0 - s))) * gain
    return r * (u - xr * jnp.mean(xr * u, axis=-1, keepdims=True))


def store_shifts(value, cols, ref, start):
    n = value.shape[0]
    col = lax.broadcasted_iota(jnp.int32, value.shape, 0) % cols
    before = jnp.where(col == 0, 0.0, pltpu.roll(value, 1, 0))
    after = jnp.where(col == cols - 1, 0.0, pltpu.roll(value, n - 1, 0))
    ref[0, start : start + n, :] = before.astype(jnp.bfloat16)
    ref[1, start : start + n, :] = value.astype(jnp.bfloat16)
    ref[2, start : start + n, :] = after.astype(jnp.bfloat16)


def kernel(
    sections, replicas, micro, rows, cols, ch, taps, own_taps, loss_scale,
    ts_ref, images, table, weight, gains, out_grad, result,
    framed, gates, yout, sout, seed, gf_in, grad_f, shift, w, wt, tab, gn, gn_last, gain_mod,
    gain_last, ts_held,
    f_all, ab_all, g_all, ft, gshift, acc,
    lsem, band_s, band_r, halo_s, halo_r, pq_s, pq_r, gf_s, gf_r, gain_s, gain_r,
    fx_s, fx_r, fh_s, fh_r, ax_s, ax_r, ah_s, ah_r, g_s, g_r,
):
    sec = lax.axis_index("section")
    d = lax.axis_index("dp")
    h = lax.axis_index("space")
    other = 1 - h
    block = sec // 2
    enc = sec % 2 == 0
    dec = jnp.logical_not(enc)
    first, last, pre = sec == 0, sec == 1, sec == 3
    turn = block == sections // 2 - 1
    follow = jnp.where(enc, jnp.where(turn, sec + 1, sec + 2), jnp.where(last, 0, sec - 2))
    ahead = jnp.where(dec, jnp.where(turn, sec - 1, sec + 2), jnp.where(first, 1, sec - 2))
    pair = jnp.where(enc, sec + 1, sec - 1)
    use_skip = jnp.logical_and(dec, jnp.logical_not(turn))
    use_gskip = jnp.logical_and(enc, jnp.logical_not(turn))
    pixels = rows * cols
    frame = pixels + 2 * cols
    peers = replicas * 2
    me = d * 2 + h
    band = pl.ds(cols, pixels)
    halo_out = pl.multiple_of(h * (pixels + cols), cols)
    halo_in = pl.multiple_of(other * (pixels + cols), cols)
    edge = pl.multiple_of(other * (pixels - cols), cols)

    def local(src, dst, i):
        return pltpu.make_async_copy(src, dst, lsem.at[i])

    def image_copy(m):
        return local(images.at[m], framed.at[X, m, band], m)

    def seed_copy(m):
        return local(out_grad.at[m], framed.at[G, m, band], micro + m)

    def pre_copy(m):
        return local(out_grad.at[m], seed.at[m], micro + m)

    ts_copy = local(ts_ref, ts_held, 2 * micro + 4)
    table_copy = local(table, tab, 2 * micro)
    gains_copy = local(gains, gn, 2 * micro + 1)
    weight_copy = local(weight, w, 2 * micro + 2)
    for m in range(micro):
        pl.when(first)(lambda m=m: image_copy(m).start())
        pl.when(last)(lambda m=m: seed_copy(m).start())
        pl.when(pre)(lambda m=m: pre_copy(m).start())
    ts_copy.start()
    table_copy.start()
    gains_copy.start()
    weight_copy.start()

    barrier = pltpu.get_barrier_semaphore()
    for s in (follow, ahead, pair):
        for side in range(2):
            pl.semaphore_signal(
                barrier, inc=1, device_id={"section": s, "space": side}, device_id_type=MESH
            )
    for k in range(1, peers):
        to = lax.rem(me + k, peers)
        pl.semaphore_signal(
            barrier, inc=1, device_id={"dp": to // 2, "space": to % 2}, device_id_type=MESH
        )

    zero_row = jnp.zeros((cols, ch), jnp.bfloat16)
    for m in range(micro):
        for kind in range(4):
            framed[kind, m, pl.ds(halo_out, cols), :] = zero_row
        for br in range(2):
            gates[m, br, pl.ds(halo_out, cols), :] = jnp.zeros((cols, ch), jnp.float32)
    for br in range(2):
        for k in range(3):
            gshift[br, k, 0:cols, :] = zero_row
            gshift[br, k, cols + 2 * pixels : 2 * cols + 2 * pixels, :] = zero_row
    acc[...] = jnp.zeros_like(acc)
    pl.semaphore_wait(barrier, 6 + peers - 1)

    def band_copy(kind, m, src, to):
        return pltpu.make_async_remote_copy(
            src, framed.at[kind, m, band], band_s.at[kind, m], band_r.at[kind, m],
            device_id={"section": to}, device_id_type=MESH,
        )

    def halo_copy(kind, m, src, to):
        return pltpu.make_async_remote_copy(
            src, framed.at[kind, m, pl.ds(halo_out, cols)],
            halo_s.at[kind, m], halo_r.at[kind, m],
            device_id={"section": to, "space": other}, device_id_type=MESH,
        )

    def sends(kind, m, src, to):
        return (
            halo_copy(kind, m, src.at[m, pl.ds(edge, cols)], to),
            band_copy(kind, m, src.at[m], to),
        )

    def rim_send(kind, m):
        src = framed.at[kind, m, pl.ds(pl.multiple_of(edge + cols, cols), cols)]
        return halo_copy(kind, m, src, sec)

    def band_wait(kind, m):
        band_copy(kind, m, yout.at[m], sec).wait_recv()

    def halo_wait(kind, m):
        pltpu.make_async_remote_copy(
            yout.at[m, pl.ds(0, cols)], framed.at[kind, m, pl.ds(halo_in, cols)],
            halo_s.at[kind, m], halo_r.at[kind, m],
            device_id={"section": sec, "space": other}, device_id_type=MESH,
        ).wait_recv()

    def pq_copy(m):
        return pltpu.make_async_remote_copy(
            gates.at[m, :, pl.ds(pl.multiple_of(edge + cols, cols), cols)],
            gates.at[m, :, pl.ds(halo_out, cols)],
            pq_s.at[m], pq_r.at[m], device_id={"space": other}, device_id_type=MESH,
        )

    def pq_wait(m):
        pltpu.make_async_remote_copy(
            gates.at[m, :, pl.ds(cols, cols)], gates.at[m, :, pl.ds(halo_in, cols)],
            pq_s.at[m], pq_r.at[m], device_id={"space": other}, device_id_type=MESH,
        ).wait_recv()

    def share(ref, send, recv, m, k):
        to = lax.rem(me + k, peers)
        return pltpu.make_async_remote_copy(
            ref.at[d * micro + m, h], ref.at[d * micro + m, h], send.at[k, m], recv.at[k, m],
            device_id={"dp": to // 2, "space": to % 2}, device_id_type=MESH,
        )

    def across(ref, send, recv, m, k):
        slot = ref.at[d * micro + m, h]
        return pltpu.make_async_remote_copy(
            slot, slot, send.at[k, m], recv.at[k, m],
            device_id={"dp": lax.rem(d + k, replicas)}, device_id_type=MESH,
        )

    def beside(ref, send, recv, m, r, side):
        slot = ref.at[r * micro + m, side]
        return pltpu.make_async_remote_copy(
            slot, slot, send.at[r, m], recv.at[r, m],
            device_id={"space": other}, device_id_type=MESH,
        )

    def start_fields(m):
        for k in range(1, replicas):
            across(f_all, fx_s, fx_r, m, k).start()
        beside(f_all, fh_s, fh_r, m, d, h).start()

        @pl.when(enc)
        def _():
            for k in range(1, replicas):
                across(ab_all, ax_s, ax_r, m, k).start()
            beside(ab_all, ah_s, ah_r, m, d, h).start()

    def hand_on(ref, xs, xr, hs, hr, m, r):
        slot = ref.at[r * micro + m, h]
        k = lax.rem(d - r + replicas, replicas)
        pltpu.make_async_remote_copy(
            slot, slot, xs.at[k, m], xr.at[k, m], device_id={"dp": r}, device_id_type=MESH
        ).wait_recv()
        beside(ref, hs, hr, m, r, h).start()

    def gf_copy(m):
        return pltpu.make_async_remote_copy(
            sout.at[0, m], gf_in.at[m], gf_s.at[m], gf_r.at[m],
            device_id={"section": ahead}, device_id_type=MESH,
        )

    def gain_copy():
        return pltpu.make_async_remote_copy(
            gn, gn_last, gain_s.at[0], gain_r.at[0],
            device_id={"section": ahead}, device_id_type=MESH,
        )

    def share_wait(ref, send, recv, m, r):
        def one(side):
            source = r * 2 + side
            k = lax.rem(me - source + peers, peers)
            slot = ref.at[r * micro + m, side]
            pltpu.make_async_remote_copy(
                slot, slot, send.at[k, m], recv.at[k, m],
                device_id={"dp": r, "space": side}, device_id_type=MESH,
            ).wait_recv()

        one(other)
        pl.when(r != d)(lambda: one(h))

    def each_micro(body):
        lax.fori_loop(0, micro, lambda m, c: (body(m), c)[1], 0)

    def start_rims():
        def images_in(m):
            image_copy(m).wait()
            rim_send(X, m).start()

        def seeds_in(m):
            seed_copy(m).wait()
            rim_send(G, m).start()

        pl.when(first)(lambda: each_micro(images_in))
        pl.when(last)(lambda: each_micro(seeds_in))

    start_rims()
    gains_copy.wait()
    pl.when(last)(lambda: gain_copy().start())
    ts_copy.wait()
    table_copy.wait()

    def modulation(m):
        return 1.0 + tab[pl.ds(ts_held[m], 1), :]

    for m in range(micro):
        gain_mod[m, :, :] = gn[...] * modulation(m)

    def gain_of(m, br):
        return gain_mod[m, pl.ds(br, 1), :]

    def wait_x(m):
        pl.when(jnp.logical_not(first))(lambda: band_wait(X, m))
        halo_wait(X, m)

    def wait_skip(m):
        @pl.when(use_skip)
        def _():
            band_wait(SKIP, m)
            halo_wait(SKIP, m)

    def inputs(m, part):
        a = framed[X, m, part, :].astype(jnp.float32)
        v = jnp.where(use_skip, framed[SKIP, m, part, :].astype(jnp.float32), a)
        return a, v

    def share_g(m):
        for k in range(1, peers):
            share(g_all, g_s, g_r, m, k).start()

    def conv(kernels, br, backward):
        pieces = []
        for t in range(9):
            i, j = t // 3, t % 3
            if backward:
                i, j = 2 - i, 2 - j
            pieces.append(shift[br, j, i * cols : i * cols + pixels, :])
        lhs = jnp.concatenate(pieces, axis=1)
        return jnp.dot(lhs, kernels[br], preferred_element_type=jnp.float32)

    def forward(m):
        wait_skip(m)
        wait_x(m)
        a, v = inputs(m, pl.ds(0, frame))
        for br, x in ((0, a), (1, v)):
            f = normalize(x, gain_of(m, br))
            store_shifts(f, cols, shift.at[br], 0)
            f_all[d * micro + m, h, br, :, :] = shift[br, 1, cols : cols + pixels, :]
        pl.when(jnp.logical_and(enc, m == 0))(weight_copy.wait)
        p = conv(w, 0, False)
        q = conv(w, 1, False)
        centre = framed[X, m, band, :].astype(jnp.float32)
        y = jnp.where(enc, centre + p * sigmoid(q), centre + p + q)
        yout[m] = y.astype(jnp.bfloat16)

        @pl.when(pre)
        def _():
            gf_copy(m).wait_recv()
            pre_copy(m).wait()
            x = yout[m].astype(jnp.float32)
            main = pull_back(x, gain_last[m, 0:1, :], gf_in[m].astype(jnp.float32))
            grad = seed[m].astype(jnp.float32) * loss_scale + main
            framed[G, m, band, :] = grad.astype(jnp.bfloat16)
            rim_send(G, m).start()

        for copy in sends(X, m, yout, follow):
            copy.start()

        @pl.when(use_gskip)
        def _():
            for copy in sends(SKIP, m, yout, pair):
                copy.start()

        @pl.when(enc)
        def _():
            slot = d * micro + m
            s = sigmoid(q)
            for br, gate in ((0, s), (1, p * s * (1.0 - s))):
                gates[m, br, band, :] = gate
                ab_all[slot, h, br, :, :] = gate.astype(jnp.bfloat16)
            pq_copy(m).start()

    def transposes():
        def one(t, c):
            at = pl.ds(pl.multiple_of(t * ch, ch), ch)
            for br in range(2):
                wt[br, at, :] = w[br, at, :].T
            return c

        lax.fori_loop(0, 9, one, 0)

    def field_grads(m):
        pl.when(jnp.logical_not(jnp.logical_or(last, pre)))(lambda: band_wait(G, m))
        halo_wait(G, m)

        @pl.when(use_gskip)
        def _():
            band_wait(GSKIP, m)
            halo_wait(GSKIP, m)

        g = out_gradient(m, pl.ds(0, frame))
        g_all[d * micro + m, h, :, :] = g[cols : cols + pixels].astype(jnp.bfloat16)
        pl.when(first)(lambda: share_g(m))

        @pl.when(jnp.logical_not(first))
        def _():
            for br in range(2):
                grad = jnp.where(enc, g * gates[m, br], g)
                store_shifts(grad, cols, shift.at[br], 0)
            for br in range(2):
                grad_f[m, br] = conv(wt, br, True)

    def out_gradient(m, part):
        g = framed[G, m, part, :].astype(jnp.float32)
        g = g + jnp.where(use_gskip, framed[GSKIP, m, part, :].astype(jnp.float32), 0.0)
        return g * jnp.where(last, loss_scale, 1.0)

    def pass_grads(m):
        a, v = inputs(m, band)
        main = pull_back(a, gain_of(m, 0), grad_f[m, 0])
        side = pull_back(v, gain_of(m, 1), grad_f[m, 1])
        g = out_gradient(m, band)
        yout_g = g + main + jnp.where(use_skip, 0.0, side)
        sout[0, m] = yout_g.astype(jnp.bfloat16)
        for copy in sends(G, m, sout.at[0], ahead):
            copy.start()

        @pl.when(use_skip)
        def _():
            sout[1, m] = side.astype(jnp.bfloat16)
            for copy in sends(GSKIP, m, sout.at[1], pair):
                copy.start()

        share_g(m)

    def last_skip(m):
        wait_skip(m)
        v = framed[SKIP, m, band, :].astype(jnp.float32)
        sout[1, m] = pull_back(v, gain_of(m, 1), grad_f[m, 1]).astype(jnp.bfloat16)
        for copy in sends(GSKIP, m, sout.at[1], pair):
            copy.start()

    def late_fields(m):
        wait_x(m)
        a, v = inputs(m, band)
        for br, x in ((0, a), (1, v)):
            f_all[d * micro + m, h, br, :, :] = normalize(x, gain_of(m, br)).astype(jnp.bfloat16)

    def gather_fields():
        def one(m):
            def pass_on(rr, c):
                r = lax.rem(d + rr, replicas)
                hand_on(f_all, fx_s, fx_r, fh_s, fh_r, m, r)
                pl.when(enc)(lambda: hand_on(ab_all, ax_s, ax_r, ah_s, ah_r, m, r))
                return c

            lax.fori_loop(1, replicas, pass_on, 0)

            def flip(rr, c):
                r = lax.rem(d + rr, replicas)
                beside(f_all, fh_s, fh_r, m, r, other).wait_recv()
                pl.when(enc)(lambda: beside(ab_all, ah_s, ah_r, m, r, other).wait_recv())
                for br in range(2):
                    for side in range(2):
                        at = slice(side * pixels, (side + 1) * pixels)
                        ft[r * micro + m, br, :, at] = f_all[r * micro + m, side, br].T
                return c

            lax.fori_loop(0, replicas, flip, 0)

        each_micro(one)

    def last_section():
        weight_copy.wait()
        transposes()

        def one(m):
            field_grads(m)
            sout[0, m] = grad_f[m, 0].astype(jnp.bfloat16)
            gf_copy(m).start()

        each_micro(one)
        each_micro(last_skip)
        each_micro(share_g)
        each_micro(late_fields)
        each_micro(start_fields)
        gather_fields()

    def other_sections():
        @pl.when(dec)
        def _():
            weight_copy.wait()
            transposes()

        @pl.when(pre)
        def _():
            gain_copy().wait_recv()
            for m in range(micro):
                gain_last[m, :, :] = gn_last[...] * modulation(m)

        each_micro(forward)

        @pl.when(enc)
        def _():
            each_micro(start_fields)
            pl.when(jnp.logical_not(first))(transposes)
            each_micro(pq_wait)
            gather_fields()

        def one(m):
            field_grads(m)
            pl.when(jnp.logical_not(first))(lambda: pass_grads(m))

        each_micro(one)

        @pl.when(dec)
        def _():
            each_micro(start_fields)
            gather_fields()

    pl.when(last)(last_section)
    pl.when(jnp.logical_not(last))(other_sections)

    own = 9 * ch // peers
    tap0 = jnp.minimum(me * own // ch, 9 - own_taps)
    offset = pl.multiple_of(me * own - tap0 * ch, 16)

    def weight_terms(m):
        def one(rr, c):
            r = lax.rem(d + rr, replicas)
            image = r * micro + m
            share_wait(g_all, g_s, g_r, m, r)
            for br in range(2):
                for side in range(2):
                    g = g_all[image, side].astype(jnp.float32)
                    gate = ab_all[image, side, br].astype(jnp.float32)
                    grad = jnp.where(enc, g * gate, g)
                    store_shifts(grad, cols, gshift.at[br], cols + side * pixels)
            for br in range(2):
                for n in range(own_taps):
                    t = tap0 + n
                    start = pl.multiple_of((2 - t // 3) * cols, cols)
                    rhs = gshift[br, 2 - t % 3, pl.ds(start, 2 * pixels), :]
                    acc[br, n * ch : (n + 1) * ch, :] += jnp.dot(
                        ft[image, br], rhs, preferred_element_type=jnp.float32
                    )
            return c

        lax.fori_loop(0, replicas, one, 0)

    each_micro(weight_terms)
    out_copy = local(acc.at[:, pl.ds(offset, own)], result, 2 * micro + 3)
    out_copy.start()

    def finish(m):
        pl.when(first)(lambda: rim_send(X, m).wait_send())
        pl.when(jnp.logical_or(last, pre))(lambda: rim_send(G, m).wait_send())
        pl.when(last)(lambda: gf_copy(m).wait_send())

        @pl.when(jnp.logical_not(last))
        def _():
            for copy in sends(X, m, yout, follow):
                copy.wait_send()

        @pl.when(enc)
        def _():
            pq_copy(m).wait_send()
            for k in range(1, replicas):
                across(ab_all, ax_s, ax_r, m, k).wait_send()
            for r in range(replicas):
                beside(ab_all, ah_s, ah_r, m, r, h).wait_send()

        @pl.when(jnp.logical_not(jnp.logical_or(first, last)))
        def _():
            for copy in sends(G, m, sout.at[0], ahead):
                copy.wait_send()

        @pl.when(use_gskip)
        def _():
            for copy in sends(SKIP, m, yout, pair):
                copy.wait_send()

        @pl.when(use_skip)
        def _():
            for copy in sends(GSKIP, m, sout.at[1], pair):
                copy.wait_send()

        for k in range(1, peers):
            share(g_all, g_s, g_r, m, k).wait_send()
        for k in range(1, replicas):
            across(f_all, fx_s, fx_r, m, k).wait_send()
        for r in range(replicas):
            beside(f_all, fh_s, fh_r, m, r, h).wait_send()

    each_micro(finish)
    pl.when(last)(lambda: gain_copy().wait_send())
    out_copy.wait()


def shards(images, timesteps, time_embed, conv_weight, norm_gain, out_grad):
    micro, rows, cols, ch = images.shape
    sections = lax.axis_size("section")
    replicas = lax.axis_size("dp")
    spaces = lax.axis_size("space")
    taps = conv_weight.shape[2]
    peers = replicas * spaces
    own = taps // peers
    own_taps = max(((n + 1) * own - 1) // ch - n * own // ch + 1 for n in range(peers))
    loss_scale = 1.0 / math.sqrt(micro * replicas * rows * spaces * cols)
    pixels = rows * cols
    frame = pixels + 2 * cols
    bf, f32 = jnp.bfloat16, jnp.float32
    dma = pltpu.SemaphoreType.DMA
    hbm_spec = pl.BlockSpec(memory_space=pltpu.HBM)
    result = pl.pallas_call(
        functools.partial(
            kernel, sections, replicas, micro, rows, cols, ch, taps, own_taps, loss_scale
        ),
        out_shape=jax.ShapeDtypeStruct((2, own, ch), f32),
        in_specs=[hbm_spec] * 6,
        out_specs=pl.BlockSpec(memory_space=pl.ANY),
        scratch_shapes=[
            pltpu.VMEM((4, micro, frame, ch), bf),
            pltpu.VMEM((micro, 2, frame, ch), f32),
            pltpu.VMEM((micro, pixels, ch), bf),
            pltpu.VMEM((2, micro, pixels, ch), bf),
            pltpu.VMEM((micro, pixels, ch), bf),
            pltpu.VMEM((micro, pixels, ch), bf),
            pltpu.VMEM((micro, 2, pixels, ch), f32),
            pltpu.VMEM((2, 3, frame, ch), bf),
            pltpu.VMEM((2, taps, ch), bf),
            pltpu.VMEM((2, taps, ch), bf),
            pltpu.VMEM(time_embed.shape, f32),
            pltpu.VMEM((2, ch), f32),
            pltpu.VMEM((2, ch), f32),
            pltpu.VMEM((micro, 2, ch), f32),
            pltpu.VMEM((micro, 2, ch), f32),
            pltpu.SMEM((micro,), jnp.int32),
            pltpu.VMEM((replicas * micro, 2, 2, pixels, ch), bf),
            pltpu.VMEM((replicas * micro, 2, 2, pixels, ch), bf),
            pltpu.VMEM((replicas * micro, 2, pixels, ch), bf),
            pltpu.VMEM((replicas * micro, 2, ch, 2 * pixels), bf),
            pltpu.VMEM((2, 3, 2 * pixels + 2 * cols, ch), bf),
            pltpu.VMEM((2, own_taps * ch, ch), f32),
            dma((2 * micro + 5,)),
            dma((4, micro)),
            dma((4, micro)),
            dma((4, micro)),
            dma((4, micro)),
            dma((micro,)),
            dma((micro,)),
            dma((micro,)),
            dma((micro,)),
            dma((1,)),
            dma((1,)),
            dma((replicas, micro)),
            dma((replicas, micro)),
            dma((replicas, micro)),
            dma((replicas, micro)),
            dma((replicas, micro)),
            dma((replicas, micro)),
            dma((replicas, micro)),
            dma((replicas, micro)),
            dma((peers, micro)),
            dma((peers, micro)),
        ],
        compiler_params=pltpu.CompilerParams(
            collective_id=0, has_side_effects=True, vmem_limit_bytes=60 * 2**20
        ),
    )(
        timesteps,
        images.reshape(micro, pixels, ch),
        time_embed,
        conv_weight[0],
        norm_gain[0],
        out_grad.reshape(micro, pixels, ch),
    )
    return result[None]


def solution(mesh):
    placed = (
        P(("groups", "dp"), "space", None, None),
        P(("groups", "dp")),
        P(),
        P("section", None, None, None),
        P("section", None, None),
        P(("groups", "dp"), "space", None, None),
    )
    return jax.shard_map(
        shards,
        mesh=mesh,
        in_specs=placed,
        out_specs=P(("groups", "section"), None, ("dp", "space"), None),
        check_vma=False,
    )
```

```python
import functools
import math

import jax
import jax.numpy as jnp
from jax import lax
from jax.experimental import pallas as pl
from jax.experimental.pallas import tpu as pltpu
from jax.sharding import PartitionSpec as P

EPSILON = 1e-06
MESH = pl.DeviceIdType.MESH
X, SKIP, G, GSKIP = range(4)


def sigmoid(z):
    return 0.5 + 0.5 * jnp.tanh(0.5 * z)


def inv_rms(x):
    return lax.rsqrt(jnp.mean(x * x, axis=-1, keepdims=True) + EPSILON)


def normalize(x, gain):
    z = x * inv_rms(x) * gain
    return z * sigmoid(z)


def pull_back(x, gain, grad_f):
    r = inv_rms(x)
    xr = x * r
    z = xr * gain
    s = sigmoid(z)
    u = grad_f * (s * (1.0 + z * (1.0 - s))) * gain
    return r * (u - xr * jnp.mean(xr * u, axis=-1, keepdims=True))


def store_shifts(value, cols, ref, start):
    n = value.shape[0]
    col = lax.broadcasted_iota(jnp.int32, value.shape, 0) % cols
    before = jnp.where(col == 0, 0.0, pltpu.roll(value, 1, 0))
    after = jnp.where(col == cols - 1, 0.0, pltpu.roll(value, n - 1, 0))
    ref[0, start : start + n, :] = before.astype(jnp.bfloat16)
    ref[1, start : start + n, :] = value.astype(jnp.bfloat16)
    ref[2, start : start + n, :] = after.astype(jnp.bfloat16)


def kernel(
    sections, replicas, micro, rows, cols, ch, taps, own_taps, loss_scale,
    ts_ref, images, table, weight, gains, out_grad, result,
    framed, gates, yout, sout, seed, gf_in, grad_f, shift, w, wt, tab, gn, gn_last, gain_mod,
    gain_last, ts_held,
    f_all, ab_all, g_all, ft, gshift, acc,
    lsem, band_s, band_r, halo_s, halo_r, pq_s, pq_r, gf_s, gf_r, gain_s, gain_r,
    fx_s, fx_r, fh_s, fh_r, ax_s, ax_r, ah_s, ah_r, g_s, g_r,
):
    sec = lax.axis_index("section")
    d = lax.axis_index("dp")
    h = lax.axis_index("space")
    other = 1 - h
    block = sec // 2
    enc = sec % 2 == 0
    dec = jnp.logical_not(enc)
    first, last, pre = sec == 0, sec == 1, sec == 3
    turn = block == sections // 2 - 1
    follow = jnp.where(enc, jnp.where(turn, sec + 1, sec + 2), jnp.where(last, 0, sec - 2))
    ahead = jnp.where(dec, jnp.where(turn, sec - 1, sec + 2), jnp.where(first, 1, sec - 2))
    pair = jnp.where(enc, sec + 1, sec - 1)
    use_skip = jnp.logical_and(dec, jnp.logical_not(turn))
    use_gskip = jnp.logical_and(enc, jnp.logical_not(turn))
    pixels = rows * cols
    frame = pixels + 2 * cols
    peers = replicas * 2
    me = d * 2 + h
    band = pl.ds(cols, pixels)
    halo_out = pl.multiple_of(h * (pixels + cols), cols)
    halo_in = pl.multiple_of(other * (pixels + cols), cols)
    edge = pl.multiple_of(other * (pixels - cols), cols)

    def local(src, dst, i):
        return pltpu.make_async_copy(src, dst, lsem.at[i])

    def image_copy(m):
        return local(images.at[m], framed.at[X, m, band], m)

    def seed_copy(m):
        return local(out_grad.at[m], framed.at[G, m, band], micro + m)

    def pre_copy(m):
        return local(out_grad.at[m], seed.at[m], micro + m)

    ts_copy = local(ts_ref, ts_held, 2 * micro + 4)
    table_copy = local(table, tab, 2 * micro)
    gains_copy = local(gains, gn, 2 * micro + 1)
    weight_copy = local(weight, w, 2 * micro + 2)
    for m in range(micro):
        pl.when(first)(lambda m=m: image_copy(m).start())
        pl.when(last)(lambda m=m: seed_copy(m).start())
        pl.when(pre)(lambda m=m: pre_copy(m).start())
    ts_copy.start()
    table_copy.start()
    gains_copy.start()
    weight_copy.start()

    barrier = pltpu.get_barrier_semaphore()
    for s in (follow, ahead, pair):
        for side in range(2):
            pl.semaphore_signal(
                barrier, inc=1, device_id={"section": s, "space": side}, device_id_type=MESH
            )
    for k in range(1, peers):
        to = lax.rem(me + k, peers)
        pl.semaphore_signal(
            barrier, inc=1, device_id={"dp": to // 2, "space": to % 2}, device_id_type=MESH
        )

    zero_row = jnp.zeros((cols, ch), jnp.bfloat16)
    for m in range(micro):
        for kind in range(4):
            framed[kind, m, pl.ds(halo_out, cols), :] = zero_row
        for br in range(2):
            gates[m, br, pl.ds(halo_out, cols), :] = jnp.zeros((cols, ch), jnp.float32)
    for br in range(2):
        for k in range(3):
            gshift[br, k, 0:cols, :] = zero_row
            gshift[br, k, cols + 2 * pixels : 2 * cols + 2 * pixels, :] = zero_row
    acc[...] = jnp.zeros_like(acc)
    pl.semaphore_wait(barrier, 6 + peers - 1)

    def band_copy(kind, m, src, to):
        return pltpu.make_async_remote_copy(
            src, framed.at[kind, m, band], band_s.at[kind, m], band_r.at[kind, m],
            device_id={"section": to}, device_id_type=MESH,
        )

    def halo_copy(kind, m, src, to):
        return pltpu.make_async_remote_copy(
            src, framed.at[kind, m, pl.ds(halo_out, cols)],
            halo_s.at[kind, m], halo_r.at[kind, m],
            device_id={"section": to, "space": other}, device_id_type=MESH,
        )

    def sends(kind, m, src, to):
        return (
            halo_copy(kind, m, src.at[m, pl.ds(edge, cols)], to),
            band_copy(kind, m, src.at[m], to),
        )

    def rim_send(kind, m):
        src = framed.at[kind, m, pl.ds(pl.multiple_of(edge + cols, cols), cols)]
        return halo_copy(kind, m, src, sec)

    def band_wait(kind, m):
        band_copy(kind, m, yout.at[m], sec).wait_recv()

    def halo_wait(kind, m):
        pltpu.make_async_remote_copy(
            yout.at[m, pl.ds(0, cols)], framed.at[kind, m, pl.ds(halo_in, cols)],
            halo_s.at[kind, m], halo_r.at[kind, m],
            device_id={"section": sec, "space": other}, device_id_type=MESH,
        ).wait_recv()

    def pq_copy(m):
        return pltpu.make_async_remote_copy(
            gates.at[m, :, pl.ds(pl.multiple_of(edge + cols, cols), cols)],
            gates.at[m, :, pl.ds(halo_out, cols)],
            pq_s.at[m], pq_r.at[m], device_id={"space": other}, device_id_type=MESH,
        )

    def pq_wait(m):
        pltpu.make_async_remote_copy(
            gates.at[m, :, pl.ds(cols, cols)], gates.at[m, :, pl.ds(halo_in, cols)],
            pq_s.at[m], pq_r.at[m], device_id={"space": other}, device_id_type=MESH,
        ).wait_recv()

    def share(ref, send, recv, m, k):
        to = lax.rem(me + k, peers)
        return pltpu.make_async_remote_copy(
            ref.at[d * micro + m, h], ref.at[d * micro + m, h], send.at[k, m], recv.at[k, m],
            device_id={"dp": to // 2, "space": to % 2}, device_id_type=MESH,
        )

    def across(ref, send, recv, m, k):
        slot = ref.at[d * micro + m, h]
        return pltpu.make_async_remote_copy(
            slot, slot, send.at[k, m], recv.at[k, m],
            device_id={"dp": lax.rem(d + k, replicas)}, device_id_type=MESH,
        )

    def beside(ref, send, recv, m, r, side):
        slot = ref.at[r * micro + m, side]
        return pltpu.make_async_remote_copy(
            slot, slot, send.at[r, m], recv.at[r, m],
            device_id={"space": other}, device_id_type=MESH,
        )

    def start_fields(m):
        for k in range(1, replicas):
            across(f_all, fx_s, fx_r, m, k).start()
        beside(f_all, fh_s, fh_r, m, d, h).start()

        @pl.when(enc)
        def _():
            for k in range(1, replicas):
                across(ab_all, ax_s, ax_r, m, k).start()
            beside(ab_all, ah_s, ah_r, m, d, h).start()

    def hand_on(ref, xs, xr, hs, hr, m, r):
        slot = ref.at[r * micro + m, h]
        k = lax.rem(d - r + replicas, replicas)
        pltpu.make_async_remote_copy(
            slot, slot, xs.at[k, m], xr.at[k, m], device_id={"dp": r}, device_id_type=MESH
        ).wait_recv()
        beside(ref, hs, hr, m, r, h).start()

    def gf_copy(m):
        return pltpu.make_async_remote_copy(
            sout.at[0, m], gf_in.at[m], gf_s.at[m], gf_r.at[m],
            device_id={"section": ahead}, device_id_type=MESH,
        )

    def gain_copy():
        return pltpu.make_async_remote_copy(
            gn, gn_last, gain_s.at[0], gain_r.at[0],
            device_id={"section": ahead}, device_id_type=MESH,
        )

    def share_wait(ref, send, recv, m, r):
        def one(side):
            source = r * 2 + side
            k = lax.rem(me - source + peers, peers)
            slot = ref.at[r * micro + m, side]
            pltpu.make_async_remote_copy(
                slot, slot, send.at[k, m], recv.at[k, m],
                device_id={"dp": r, "space": side}, device_id_type=MESH,
            ).wait_recv()

        one(other)
        pl.when(r != d)(lambda: one(h))

    def each_micro(body):
        lax.fori_loop(0, micro, lambda m, c: (body(m), c)[1], 0)

    def start_rims():
        def images_in(m):
            image_copy(m).wait()
            rim_send(X, m).start()

        def seeds_in(m):
            seed_copy(m).wait()
            rim_send(G, m).start()

        pl.when(first)(lambda: each_micro(images_in))
        pl.when(last)(lambda: each_micro(seeds_in))

    start_rims()
    gains_copy.wait()
    pl.when(last)(lambda: gain_copy().start())
    ts_copy.wait()
    table_copy.wait()

    def modulation(m):
        return 1.0 + tab[pl.ds(ts_held[m], 1), :]

    for m in range(micro):
        gain_mod[m, :, :] = gn[...] * modulation(m)

    def gain_of(m, br):
        return gain_mod[m, pl.ds(br, 1), :]

    def wait_x(m):
        pl.when(jnp.logical_not(first))(lambda: band_wait(X, m))
        halo_wait(X, m)

    def wait_skip(m):
        @pl.when(use_skip)
        def _():
            band_wait(SKIP, m)
            halo_wait(SKIP, m)

    def inputs(m, part):
        a = framed[X, m, part, :].astype(jnp.float32)
        v = jnp.where(use_skip, framed[SKIP, m, part, :].astype(jnp.float32), a)
        return a, v

    def share_g(m):
        for k in range(1, peers):
            share(g_all, g_s, g_r, m, k).start()

    def conv(kernels, br, backward):
        pieces = []
        for t in range(9):
            i, j = t // 3, t % 3
            if backward:
                i, j = 2 - i, 2 - j
            pieces.append(shift[br, j, i * cols : i * cols + pixels, :])
        lhs = jnp.concatenate(pieces, axis=1)
        return jnp.dot(lhs, kernels[br], preferred_element_type=jnp.float32)

    def forward(m):
        wait_skip(m)
        wait_x(m)
        a, v = inputs(m, pl.ds(0, frame))
        for br, x in ((0, a), (1, v)):
            f = normalize(x, gain_of(m, br))
            store_shifts(f, cols, shift.at[br], 0)
            f_all[d * micro + m, h, br, :, :] = shift[br, 1, cols : cols + pixels, :]
        pl.when(jnp.logical_and(enc, m == 0))(weight_copy.wait)
        p = conv(w, 0, False)
        q = conv(w, 1, False)
        centre = framed[X, m, band, :].astype(jnp.float32)
        y = jnp.where(enc, centre + p * sigmoid(q), centre + p + q)
        yout[m] = y.astype(jnp.bfloat16)

        @pl.when(pre)
        def _():
            gf_copy(m).wait_recv()
            pre_copy(m).wait()
            x = yout[m].astype(jnp.float32)
            main = pull_back(x, gain_last[m, 0:1, :], gf_in[m].astype(jnp.float32))
            grad = seed[m].astype(jnp.float32) * loss_scale + main
            framed[G, m, band, :] = grad.astype(jnp.bfloat16)
            rim_send(G, m).start()

        for copy in sends(X, m, yout, follow):
            copy.start()

        @pl.when(enc)
        def _():
            slot = d * micro + m
            s = sigmoid(q)
            for br, gate in ((0, s), (1, p * s * (1.0 - s))):
                gates[m, br, band, :] = gate
                ab_all[slot, h, br, :, :] = gate.astype(jnp.bfloat16)
            pq_copy(m).start()

    def send_skip(m):
        @pl.when(use_gskip)
        def _():
            for copy in sends(SKIP, m, yout, pair):
                copy.start()

    def transposes():
        def one(t, c):
            at = pl.ds(pl.multiple_of(t * ch, ch), ch)
            for br in range(2):
                wt[br, at, :] = w[br, at, :].T
            return c

        lax.fori_loop(0, 9, one, 0)

    def field_grads(m):
        pl.when(jnp.logical_not(jnp.logical_or(last, pre)))(lambda: band_wait(G, m))
        halo_wait(G, m)

        @pl.when(use_gskip)
        def _():
            band_wait(GSKIP, m)
            halo_wait(GSKIP, m)

        g = out_gradient(m, pl.ds(0, frame))
        g_all[d * micro + m, h, :, :] = g[cols : cols + pixels].astype(jnp.bfloat16)
        pl.when(first)(lambda: share_g(m))

        @pl.when(jnp.logical_not(first))
        def _():
            for br in range(2):
                grad = jnp.where(enc, g * gates[m, br], g)
                store_shifts(grad, cols, shift.at[br], 0)
            for br in range(2):
                grad_f[m, br] = conv(wt, br, True)

    def out_gradient(m, part):
        g = framed[G, m, part, :].astype(jnp.float32)
        g = g + jnp.where(use_gskip, framed[GSKIP, m, part, :].astype(jnp.float32), 0.0)
        return g * jnp.where(last, loss_scale, 1.0)

    def pass_grads(m):
        a, v = inputs(m, band)
        main = pull_back(a, gain_of(m, 0), grad_f[m, 0])
        side = pull_back(v, gain_of(m, 1), grad_f[m, 1])
        g = out_gradient(m, band)
        yout_g = g + main + jnp.where(use_skip, 0.0, side)
        sout[0, m] = yout_g.astype(jnp.bfloat16)
        for copy in sends(G, m, sout.at[0], ahead):
            copy.start()

        @pl.when(use_skip)
        def _():
            sout[1, m] = side.astype(jnp.bfloat16)
            for copy in sends(GSKIP, m, sout.at[1], pair):
                copy.start()


    def last_skip(m):
        wait_skip(m)
        v = framed[SKIP, m, band, :].astype(jnp.float32)
        sout[1, m] = pull_back(v, gain_of(m, 1), grad_f[m, 1]).astype(jnp.bfloat16)
        for copy in sends(GSKIP, m, sout.at[1], pair):
            copy.start()

    def late_fields(m):
        wait_x(m)
        a, v = inputs(m, band)
        for br, x in ((0, a), (1, v)):
            f_all[d * micro + m, h, br, :, :] = normalize(x, gain_of(m, br)).astype(jnp.bfloat16)

    def gather_fields():
        def one(m):
            def pass_on(rr, c):
                r = lax.rem(d + rr, replicas)
                hand_on(f_all, fx_s, fx_r, fh_s, fh_r, m, r)
                pl.when(enc)(lambda: hand_on(ab_all, ax_s, ax_r, ah_s, ah_r, m, r))
                return c

            lax.fori_loop(1, replicas, pass_on, 0)

            def flip(rr, c):
                r = lax.rem(d + rr, replicas)
                beside(f_all, fh_s, fh_r, m, r, other).wait_recv()
                pl.when(enc)(lambda: beside(ab_all, ah_s, ah_r, m, r, other).wait_recv())
                for br in range(2):
                    for side in range(2):
                        at = slice(side * pixels, (side + 1) * pixels)
                        ft[r * micro + m, br, :, at] = f_all[r * micro + m, side, br].T
                return c

            lax.fori_loop(0, replicas, flip, 0)

        each_micro(one)

    def last_section():
        weight_copy.wait()
        transposes()

        def one(m):
            field_grads(m)
            sout[0, m] = grad_f[m, 0].astype(jnp.bfloat16)
            gf_copy(m).start()

        each_micro(one)
        each_micro(last_skip)
        each_micro(share_g)
        each_micro(late_fields)
        each_micro(start_fields)
        gather_fields()

    def other_sections():
        @pl.when(dec)
        def _():
            weight_copy.wait()
            transposes()

        @pl.when(pre)
        def _():
            gain_copy().wait_recv()
            for m in range(micro):
                gain_last[m, :, :] = gn_last[...] * modulation(m)

        each_micro(forward)

        @pl.when(enc)
        def _():
            each_micro(send_skip)
            each_micro(start_fields)
            pl.when(jnp.logical_not(first))(transposes)
            each_micro(pq_wait)
            gather_fields()

        def one(m):
            field_grads(m)
            pl.when(jnp.logical_not(first))(lambda: pass_grads(m))

        each_micro(one)
        pl.when(jnp.logical_not(first))(lambda: each_micro(share_g))

        @pl.when(dec)
        def _():
            each_micro(start_fields)
            gather_fields()

    pl.when(last)(last_section)
    pl.when(jnp.logical_not(last))(other_sections)

    own = 9 * ch // peers
    tap0 = jnp.minimum(me * own // ch, 9 - own_taps)
    offset = pl.multiple_of(me * own - tap0 * ch, 16)

    def weight_terms(m):
        def one(rr, c):
            r = lax.rem(d + rr, replicas)
            image = r * micro + m
            share_wait(g_all, g_s, g_r, m, r)
            for br in range(2):
                for side in range(2):
                    g = g_all[image, side].astype(jnp.float32)
                    gate = ab_all[image, side, br].astype(jnp.float32)
                    grad = jnp.where(enc, g * gate, g)
                    store_shifts(grad, cols, gshift.at[br], cols + side * pixels)
            for br in range(2):
                for n in range(own_taps):
                    t = tap0 + n
                    start = pl.multiple_of((2 - t // 3) * cols, cols)
                    rhs = gshift[br, 2 - t % 3, pl.ds(start, 2 * pixels), :]
                    acc[br, n * ch : (n + 1) * ch, :] += jnp.dot(
                        ft[image, br], rhs, preferred_element_type=jnp.float32
                    )
            return c

        lax.fori_loop(0, replicas, one, 0)

    each_micro(weight_terms)
    out_copy = local(acc.at[:, pl.ds(offset, own)], result, 2 * micro + 3)
    out_copy.start()

    def finish(m):
        pl.when(first)(lambda: rim_send(X, m).wait_send())
        pl.when(jnp.logical_or(last, pre))(lambda: rim_send(G, m).wait_send())
        pl.when(last)(lambda: gf_copy(m).wait_send())

        @pl.when(jnp.logical_not(last))
        def _():
            for copy in sends(X, m, yout, follow):
                copy.wait_send()

        @pl.when(enc)
        def _():
            pq_copy(m).wait_send()
            for k in range(1, replicas):
                across(ab_all, ax_s, ax_r, m, k).wait_send()
            for r in range(replicas):
                beside(ab_all, ah_s, ah_r, m, r, h).wait_send()

        @pl.when(jnp.logical_not(jnp.logical_or(first, last)))
        def _():
            for copy in sends(G, m, sout.at[0], ahead):
                copy.wait_send()

        @pl.when(use_gskip)
        def _():
            for copy in sends(SKIP, m, yout, pair):
                copy.wait_send()

        @pl.when(use_skip)
        def _():
            for copy in sends(GSKIP, m, sout.at[1], pair):
                copy.wait_send()

        for k in range(1, peers):
            share(g_all, g_s, g_r, m, k).wait_send()
        for k in range(1, replicas):
            across(f_all, fx_s, fx_r, m, k).wait_send()
        for r in range(replicas):
            beside(f_all, fh_s, fh_r, m, r, h).wait_send()

    each_micro(finish)
    pl.when(last)(lambda: gain_copy().wait_send())
    out_copy.wait()


def shards(images, timesteps, time_embed, conv_weight, norm_gain, out_grad):
    micro, rows, cols, ch = images.shape
    sections = lax.axis_size("section")
    replicas = lax.axis_size("dp")
    spaces = lax.axis_size("space")
    taps = conv_weight.shape[2]
    peers = replicas * spaces
    own = taps // peers
    own_taps = max(((n + 1) * own - 1) // ch - n * own // ch + 1 for n in range(peers))
    loss_scale = 1.0 / math.sqrt(micro * replicas * rows * spaces * cols)
    pixels = rows * cols
    frame = pixels + 2 * cols
    bf, f32 = jnp.bfloat16, jnp.float32
    dma = pltpu.SemaphoreType.DMA
    hbm_spec = pl.BlockSpec(memory_space=pltpu.HBM)
    result = pl.pallas_call(
        functools.partial(
            kernel, sections, replicas, micro, rows, cols, ch, taps, own_taps, loss_scale
        ),
        out_shape=jax.ShapeDtypeStruct((2, own, ch), f32),
        in_specs=[hbm_spec] * 6,
        out_specs=pl.BlockSpec(memory_space=pl.ANY),
        scratch_shapes=[
            pltpu.VMEM((4, micro, frame, ch), bf),
            pltpu.VMEM((micro, 2, frame, ch), f32),
            pltpu.VMEM((micro, pixels, ch), bf),
            pltpu.VMEM((2, micro, pixels, ch), bf),
            pltpu.VMEM((micro, pixels, ch), bf),
            pltpu.VMEM((micro, pixels, ch), bf),
            pltpu.VMEM((micro, 2, pixels, ch), f32),
            pltpu.VMEM((2, 3, frame, ch), bf),
            pltpu.VMEM((2, taps, ch), bf),
            pltpu.VMEM((2, taps, ch), bf),
            pltpu.VMEM(time_embed.shape, f32),
            pltpu.VMEM((2, ch), f32),
            pltpu.VMEM((2, ch), f32),
            pltpu.VMEM((micro, 2, ch), f32),
            pltpu.VMEM((micro, 2, ch), f32),
            pltpu.SMEM((micro,), jnp.int32),
            pltpu.VMEM((replicas * micro, 2, 2, pixels, ch), bf),
            pltpu.VMEM((replicas * micro, 2, 2, pixels, ch), bf),
            pltpu.VMEM((replicas * micro, 2, pixels, ch), bf),
            pltpu.VMEM((replicas * micro, 2, ch, 2 * pixels), bf),
            pltpu.VMEM((2, 3, 2 * pixels + 2 * cols, ch), bf),
            pltpu.VMEM((2, own_taps * ch, ch), f32),
            dma((2 * micro + 5,)),
            dma((4, micro)),
            dma((4, micro)),
            dma((4, micro)),
            dma((4, micro)),
            dma((micro,)),
            dma((micro,)),
            dma((micro,)),
            dma((micro,)),
            dma((1,)),
            dma((1,)),
            dma((replicas, micro)),
            dma((replicas, micro)),
            dma((replicas, micro)),
            dma((replicas, micro)),
            dma((replicas, micro)),
            dma((replicas, micro)),
            dma((replicas, micro)),
            dma((replicas, micro)),
            dma((peers, micro)),
            dma((peers, micro)),
        ],
        compiler_params=pltpu.CompilerParams(
            collective_id=0, has_side_effects=True, vmem_limit_bytes=60 * 2**20
        ),
    )(
        timesteps,
        images.reshape(micro, pixels, ch),
        time_embed,
        conv_weight[0],
        norm_gain[0],
        out_grad.reshape(micro, pixels, ch),
    )
    return result[None]


def solution(mesh):
    placed = (
        P(("groups", "dp"), "space", None, None),
        P(("groups", "dp")),
        P(),
        P("section", None, None, None),
        P("section", None, None),
        P(("groups", "dp"), "space", None, None),
    )
    return jax.shard_map(
        shards,
        mesh=mesh,
        in_specs=placed,
        out_specs=P(("groups", "section"), None, ("dp", "space"), None),
        check_vma=False,
    )
```
